256 devices in a mesh: seq: 8 (over x, core), head: 32 (over y, z).
Axes of the slice: x: 4, y: 4, z: 8, core: 2. Of those that a mesh axis runs over, the one named last changes fastest.
Arguments:
- queries: bfloat16 [32768, 4096], P(('seq', 'head')), may hold values from -4 to 4
- keys: bfloat16 [32768, 1024], P(('seq', 'head')), may hold values from -4 to 4
- values: bfloat16 [32768, 1024], P(('seq', 'head')), may hold values from -6 to 6
- modality: int32 [32768], P(('seq', 'head')), may hold values 0 or 1
- clip_lengths: int32 [128], replicated, may hold values from 1 to 512, 32768 in all
- query_gains: float32 [2, 4096], replicated, may hold values from 0.5 to 5.2
- key_gains: float32 [2, 1024], replicated, may hold values from 0.5 to 5.2
- out_grad: bfloat16 [32768, 4096], P(('seq', 'head')), may hold values from -6 to 6
Outputs:
- attended: bfloat16 [32768, 4096], P(('seq', 'head'))
- query_grad: bfloat16 [32768, 4096], P(('seq', 'head'))
- key_grad: bfloat16 [32768, 1024], P(('seq', 'head'))
- value_grad: bfloat16 [32768, 1024], P(('seq', 'head'))
- query_gain_grad: float32 [2, 4096], replicated
- key_gain_grad: float32 [2, 1024], replicated
The draws below stay inside these ranges and needn't reach their ends.
Inputs may be any that keep to these rules, and one draw needn't show every extreme that they name: `clip_lengths`: the clips cover the 32768 positions end to end; some clip has exactly 512 positions.
All inputs are finite; a program needn't handle non-finite values. No bound on the sum of `modality` on one device may be relied on, other than what follows from the above.
Results may differ from the reference program's by a relative error of at most 0.025.
The reference program's roundings to bfloat16 on the way count: a program that leaves them out, or rounds other values in their place, can miss the bound.
Values may be sent and summed in bfloat16 or wider, within the bound.
No kernel may reach another device: no remote copies, remote signals or barrier semaphores. Data moves between devices by JAX's collectives and lax.ppermute only.
A program may use at most 128 MiB of HBM per device.

```python
import math
import jax
import jax.numpy as jnp
import numpy as np
from jax import lax

H = 32
KV = 8
HD = 128
MOST = 512
TOKENS = 32768
CLIPS = 128


def draw_queries(key, part):
    key = jax.random.fold_in(key, 1)
    rows = jax.random.normal(key, (TOKENS, H * HD), jnp.float32)
    return jnp.clip(rows, -4.0, 4.0).astype(jnp.bfloat16)


def draw_keys(key, part):
    key = jax.random.fold_in(key, 2)
    rows = jax.random.normal(key, (TOKENS, KV * HD), jnp.float32)
    return jnp.clip(rows, -4.0, 4.0).astype(jnp.bfloat16)


def gain_table(key, heads):
    logs = jax.random.uniform(key, (2, heads * HD), jnp.float32, -0.6931472, 0.6931472)
    return jnp.exp(logs)


def draw_query_gains(key, part):
    key = jax.random.fold_in(key, 5)
    return gain_table(key, H)


def draw_key_gains(key, part):
    key = jax.random.fold_in(key, 6)
    return gain_table(key, KV)


def touch_ends(result, own_key, least, largest):
    longest = result.shape.index(max(result.shape))
    spots = []
    for shift in (0, 1):
        where = [jax.random.randint(jax.random.fold_in(own_key, axis), (), 0, length) for axis, length in enumerate(result.shape)]
        where[longest] = (where[longest] + shift) % result.shape[longest]
        spots.append(tuple(where))
    return result.at[spots[0]].set(least).at[spots[1]].set(largest)


def shard_levels(rng, shape, shards, least, high):
    def one(position, blocks):
        draws = jax.random.uniform(jax.random.fold_in(jax.random.fold_in(rng, 6), position), (blocks,), jnp.float32, least / len(shards), high / len(shards))
        return jnp.repeat(jnp.exp(draws), shape[position] // blocks).reshape((-1,) + (1,) * (len(shape) - position - 1))

    loudness = one(*shards[0])
    for cut in shards[1:]:
        loudness = loudness * one(*cut)
    return loudness


def profile(amount, total, most, slope):
    loads = [(1 << 20) // math.isqrt(grade ** slope) + 1 for grade in range(2, amount + 1)]
    rest, holding = total - most - (amount - 1), [1] * (amount - 1)
    while rest > 0:
        candidates = [i for i in range(amount - 1) if holding[i] < most]
        pool, remaining = sum([loads[i] for i in candidates]), rest
        for i in candidates:
            extra = min(most - holding[i], max(1, remaining * loads[i] // pool), rest)
            holding[i] = holding[i] + extra
            rest = rest - extra
    return np.array([most] + holding)


def ragged(stream_key, count, total, most, skew):
    if count == 2:
        one = jax.random.randint(stream_key, (), max(1, total - most), min(most, total - 1) + 1)
        return jnp.stack([one, total - one])
    tallies = jnp.asarray(profile(count, total, most, skew), jnp.int32)
    pairs = (count - 1) // 2
    source_of, receiver = tallies[1:1 + 2 * pairs:2], tallies[2:2 + 2 * pairs:2]
    slack = jnp.minimum(source_of - 1, most - receiver)
    shifted = jax.random.randint(jax.random.fold_in(stream_key, 1), (pairs,), 0, 1 << 20) % (slack + 1)
    tallies = tallies.at[1:1 + 2 * pairs:2].set(source_of - shifted).at[2:2 + 2 * pairs:2].set(receiver + shifted)
    return tallies[jax.random.permutation(jax.random.fold_in(stream_key, 2), count)]


def noise(key, shape, scale, bound, shards=(), held_as=jnp.bfloat16):
    gain = shard_levels(key, shape, shards, -0.22, 0.18) if shards else 1.0
    entries = jax.random.normal(key, shape, jnp.float32) * scale * gain
    return jnp.minimum(jnp.maximum(entries, -bound), bound).astype(held_as)


def setup_inputs(seed: int = 0) -> dict:
    arg_keys = jax.random.split(jax.random.key(seed), 9)
    return {
        "queries": draw_queries(jax.random.fold_in(arg_keys[8], 71), 0),
        "keys": draw_keys(jax.random.fold_in(arg_keys[8], 71), 0),
        "values": noise(arg_keys[2], (TOKENS, KV * HD), 1.0, 6.0, ((0, 256),)),
        "modality": touch_ends((jax.random.randint(arg_keys[3], (TOKENS,), 0, 3) < 1).astype(jnp.int32), jax.random.fold_in(arg_keys[3], 1), 0, 1),
        "clip_lengths": ragged(arg_keys[4], CLIPS, TOKENS, MOST, 2).astype(jnp.int32),
        "query_gains": draw_query_gains(jax.random.fold_in(arg_keys[8], 71), 0),
        "key_gains": draw_key_gains(jax.random.fold_in(arg_keys[8], 71), 0),
        "out_grad": noise(arg_keys[7], (TOKENS, H * HD), 1.0, 6.0, ((0, 256),)),
    }


row_block = 512
highest = lax.Precision.HIGHEST

def clip_start(clip_lengths, positions):
    ends = jnp.cumsum(clip_lengths, dtype=jnp.int32)
    begins = ends - clip_lengths
    chosen = jnp.where(begins[None, :] <= positions[:, None], begins[None, :], jnp.zeros((), jnp.int32))
    return lax.optimization_barrier(jnp.max(chosen, axis=1)).astype(jnp.int32)

def normalize(rows, modality, gains):
    count, width = rows.shape
    shaped = rows.astype(jnp.float32).reshape(count, width // HD, HD)
    factor = lax.rsqrt(lax.optimization_barrier(jnp.mean(shaped * shaped, axis=2, keepdims=True)) + 1e-06)
    unit = shaped * factor
    gain_rows = jnp.where(modality[:, None] == 1, gains[1][None, :], gains[0][None, :]).reshape(count, width // HD, HD)
    normed = (unit * gain_rows).astype(jnp.bfloat16).reshape(count, width)
    return (normed, unit, factor, gain_rows)

def unnormalize(grad_low, unit, factor, gain_rows, modality):
    count = unit.shape[0]
    shaped = grad_low.astype(jnp.float32).reshape(unit.shape)
    along = shaped * gain_rows
    back = factor * (along - unit * lax.optimization_barrier(jnp.mean(along * unit, axis=2, keepdims=True)))
    term = (shaped * unit).reshape(count, -1)
    choose = (modality[:, None] == jnp.arange(2, dtype=jnp.int32)[None, :]).astype(jnp.float32)
    gain_part = jnp.einsum('rm,rc->mc', choose, term, precision=highest)
    return (back.reshape(count, -1).astype(jnp.bfloat16), gain_part)

def attend(query_norm, key_ext, value_ext, grad_rows, first, starts, block):
    rows = query_norm.shape[0]
    reach = key_ext.shape[0] - rows
    span = block + reach
    scale = 1.0 / math.sqrt(query_norm.shape[2])
    offsets = jnp.arange(span, dtype=jnp.int32)
    inside = jnp.arange(block, dtype=jnp.int32)

    def visit(carry, index):
        key_acc, value_acc = carry
        begin = index * block
        query_part = lax.dynamic_slice_in_dim(query_norm, begin, block, 0).astype(jnp.float32)
        grad_part = lax.dynamic_slice_in_dim(grad_rows, begin, block, 0).astype(jnp.float32)
        key_part = lax.dynamic_slice_in_dim(key_ext, begin, span, 0).astype(jnp.float32)
        value_part = lax.dynamic_slice_in_dim(value_ext, begin, span, 0).astype(jnp.float32)
        start_part = lax.dynamic_slice_in_dim(starts, begin, block, 0)
        query_pos = first + begin + inside
        key_pos = first + begin - reach + offsets
        allowed = (key_pos[None, :] >= start_part[:, None]) & (key_pos[None, :] <= query_pos[:, None])
        scores = jnp.einsum('qnd,knd->qnk', query_part, key_part, precision=highest) * scale
        scores = jnp.where(allowed[:, None, :], scores, jnp.float32(-1e+30))
        top = lax.optimization_barrier(jnp.max(scores, axis=2, keepdims=True))
        expo = jnp.exp(scores - top)
        probs = expo / lax.optimization_barrier(jnp.sum(expo, axis=2, keepdims=True))
        probs_low = probs.astype(jnp.bfloat16).astype(jnp.float32)
        attended = jnp.einsum('qnk,knd->qnd', probs_low, value_part, precision=highest).astype(jnp.bfloat16)
        delta = lax.optimization_barrier(jnp.sum(grad_part * attended.astype(jnp.float32), axis=2, keepdims=True))
        prob_grad = jnp.einsum('qnd,knd->qnk', grad_part, value_part, precision=highest)
        score_grad = (probs * (prob_grad - delta) * scale).astype(jnp.bfloat16).astype(jnp.float32)
        query_grad = jnp.einsum('qnk,knd->qnd', score_grad, key_part, precision=highest).astype(jnp.bfloat16)
        key_step = jnp.einsum('qnk,qnd->knd', score_grad, query_part, precision=highest)
        value_step = jnp.einsum('qnk,qnd->knd', probs_low, grad_part, precision=highest)
        key_acc = lax.dynamic_update_slice_in_dim(key_acc, lax.dynamic_slice_in_dim(key_acc, begin, span, 0) + key_step, begin, 0)
        value_acc = lax.dynamic_update_slice_in_dim(value_acc, lax.dynamic_slice_in_dim(value_acc, begin, span, 0) + value_step, begin, 0)
        return ((key_acc, value_acc), (attended, query_grad))
    zeros = jnp.zeros(key_ext.shape, jnp.float32)
    (key_acc, value_acc), (attended, query_grad) = lax.scan(visit, (zeros, zeros), jnp.arange(rows // block, dtype=jnp.int32))
    heads, depth = (query_norm.shape[1], query_norm.shape[2])
    return (attended.reshape(rows, heads, depth), query_grad.reshape(rows, heads, depth), key_acc, value_acc)

def reference(queries, keys, values, modality, clip_lengths, query_gains, key_gains, out_grad):
    tokens, width = queries.shape
    kv_heads = keys.shape[1] // HD
    repeat = width // HD // kv_heads
    starts = clip_start(clip_lengths, jnp.arange(tokens, dtype=jnp.int32))
    block = min(row_block, tokens)

    def per_group(index):
        query_begin = index * repeat * HD
        key_begin = index * HD
        query_rows = lax.dynamic_slice_in_dim(queries, query_begin, repeat * HD, 1)
        grad_rows = lax.dynamic_slice_in_dim(out_grad, query_begin, repeat * HD, 1)
        key_rows = lax.dynamic_slice_in_dim(keys, key_begin, HD, 1)
        value_rows = lax.dynamic_slice_in_dim(values, key_begin, HD, 1)
        query_part_gains = lax.dynamic_slice_in_dim(query_gains, query_begin, repeat * HD, 1)
        key_part_gains = lax.dynamic_slice_in_dim(key_gains, key_begin, HD, 1)
        query_norm, query_unit, query_factor, query_gain_rows = normalize(query_rows, modality, query_part_gains)
        key_norm, key_unit, key_factor, key_gain_rows = normalize(key_rows, modality, key_part_gains)
        padding = jnp.zeros((MOST, HD), jnp.bfloat16)
        key_ext = jnp.broadcast_to(jnp.concatenate([padding, key_norm], 0).reshape(MOST + tokens, 1, HD), (MOST + tokens, repeat, HD))
        value_ext = jnp.broadcast_to(jnp.concatenate([padding, value_rows], 0).reshape(MOST + tokens, 1, HD), (MOST + tokens, repeat, HD))
        attended, query_low, key_acc, value_acc = attend(query_norm.reshape(tokens, repeat, HD), key_ext, value_ext, grad_rows.reshape(tokens, repeat, HD), jnp.zeros((), jnp.int32), starts, block)
        key_low = lax.optimization_barrier(jnp.sum(key_acc[MOST:], axis=1)).astype(jnp.bfloat16)
        value_grad = lax.optimization_barrier(jnp.sum(value_acc[MOST:], axis=1)).astype(jnp.bfloat16)
        query_grad, query_gain = unnormalize(query_low.reshape(tokens, repeat * HD), query_unit, query_factor, query_gain_rows, modality)
        key_grad, key_gain = unnormalize(key_low, key_unit, key_factor, key_gain_rows, modality)
        return (attended.reshape(tokens, repeat * HD), query_grad, key_grad, value_grad, query_gain, key_gain)
    results = lax.map(per_group, jnp.arange(kv_heads, dtype=jnp.int32))

    def flatten(stacked):
        return jnp.transpose(stacked, (1, 0, 2)).reshape(stacked.shape[1], -1)
    return (flatten(results[0]), flatten(results[1]), flatten(results[2]), flatten(results[3]), flatten(results[4]), flatten(results[5]))
```

```python
import math

import jax
import jax.numpy as jnp
from jax import lax
from jax.sharding import PartitionSpec as P

HD = 128
MOST = 512


row_block = 512


def from_behind(value, axis, steps):
    count = lax.axis_size(axis)
    first, last = (max(0, -steps), min(count, count - steps))
    return lax.ppermute(value, axis, [(source, source + steps) for source in range(first, last)])


def clip_start(clip_lengths, positions):
    order = jnp.arange(clip_lengths.shape[0], dtype=jnp.int32)
    begins = jnp.sum(jnp.where(order[None, :] < order[:, None], clip_lengths[None, :], 0), axis=1)
    chosen = jnp.where(
        begins[None, :] <= positions[:, None], begins[None, :], jnp.zeros((), jnp.int32)
    )
    return jnp.max(chosen, axis=1)


def normalize(rows, modality, gains):
    count, width = rows.shape
    shaped = rows.astype(jnp.float32).reshape(count, width // HD, HD)
    factor = lax.rsqrt(jnp.mean(shaped * shaped, axis=2, keepdims=True) + 1e-06)
    unit = shaped * factor
    gain_rows = jnp.where(modality[:, None] == 1, gains[1][None, :], gains[0][None, :]).reshape(
        count, width // HD, HD
    )
    normed = (unit * gain_rows).astype(jnp.bfloat16).reshape(count, width)
    return (normed, unit, factor, gain_rows)


def unnormalize(grad_low, unit, factor, gain_rows, modality):
    count = unit.shape[0]
    shaped = grad_low.astype(jnp.float32).reshape(unit.shape)
    along = shaped * gain_rows
    back = factor * (along - unit * jnp.mean(along * unit, axis=2, keepdims=True))
    term = (shaped * unit).reshape(count, -1)
    choose = (modality[:, None] == jnp.arange(2, dtype=jnp.int32)[None, :]).astype(jnp.float32)
    gain_part = jnp.einsum("rm,rc->mc", choose, term, precision=lax.Precision.HIGHEST)
    return (back.reshape(count, -1).astype(jnp.bfloat16), gain_part)


def spread_heads(rows, kv_heads, repeat):
    count = rows.shape[0]
    return jnp.broadcast_to(
        rows.reshape(count, kv_heads, 1, HD), (count, kv_heads, repeat, HD)
    ).reshape(count, kv_heads * repeat, HD)


def fold_heads(rows, kv_heads, repeat):
    count = rows.shape[0]
    return jnp.sum(rows.reshape(count, kv_heads, repeat, HD), axis=2)


def attend(query_norm, key_ext, value_ext, grad_rows, first, starts, block):
    rows = query_norm.shape[0]
    reach = key_ext.shape[0] - rows
    span = block + reach
    scale = 1.0 / math.sqrt(query_norm.shape[2])
    offsets = jnp.arange(span, dtype=jnp.int32)
    inside = jnp.arange(block, dtype=jnp.int32)

    def visit(carry, index):
        key_acc, value_acc = carry
        begin = index * block
        query_pos = first + begin + inside
        key_pos = first + begin - reach + offsets
        allowed = (key_pos[None, :] >= starts[:, None]) & (key_pos[None, :] <= query_pos[:, None])
        scores = (
            jnp.einsum("qnd,knd->qnk", query_norm, key_ext, preferred_element_type=jnp.float32)
            * scale
        )
        scores = jnp.where(allowed[:, None, :], scores, jnp.float32(-1e30))
        top = jnp.max(scores, axis=2, keepdims=True)
        expo = jnp.exp(scores - top)
        probs = expo / jnp.sum(expo, axis=2, keepdims=True)
        probs_low = probs.astype(jnp.bfloat16)
        attended = jnp.einsum(
            "qnk,knd->qnd", probs_low, value_ext, preferred_element_type=jnp.float32
        ).astype(jnp.bfloat16)
        delta = jnp.sum(
            grad_rows.astype(jnp.float32) * attended.astype(jnp.float32), axis=2, keepdims=True
        )
        prob_grad = jnp.einsum(
            "qnd,knd->qnk", grad_rows, value_ext, preferred_element_type=jnp.float32
        )
        score_grad = (probs * (prob_grad - delta) * scale).astype(jnp.bfloat16)
        query_grad = jnp.einsum(
            "qnk,knd->qnd", score_grad, key_ext, preferred_element_type=jnp.float32
        ).astype(jnp.bfloat16)
        key_step = jnp.einsum(
            "qnk,qnd->knd", score_grad, query_norm, preferred_element_type=jnp.float32
        )
        value_step = jnp.einsum(
            "qnk,qnd->knd", probs_low, grad_rows, preferred_element_type=jnp.float32
        )
        key_acc = key_acc + key_step
        value_acc = value_acc + value_step
        return ((key_acc, value_acc), (attended, query_grad))

    zeros = jnp.zeros(key_ext.shape, jnp.float32)
    (key_acc, value_acc), (attended, query_grad) = lax.scan(
        visit, (zeros, zeros), jnp.arange(rows // block, dtype=jnp.int32)
    )
    heads, depth = (query_norm.shape[1], query_norm.shape[2])
    return (
        attended.reshape(rows, heads, depth),
        query_grad.reshape(rows, heads, depth),
        key_acc,
        value_acc,
    )


def on_device(queries, keys, values, modality, clip_lengths, query_gains, key_gains, out_grad):
    count, width = queries.shape
    heads = width // HD
    kv_heads = keys.shape[1] // HD
    repeat = heads // kv_heads
    query_norm, query_unit, query_factor, query_gain_rows = normalize(
        queries, modality, query_gains
    )
    key_norm, key_unit, key_factor, key_gain_rows = normalize(keys, modality, key_gains)
    first = lax.axis_index(("seq", "head")) * count
    depth = (MOST + count - 1) // count
    far_keys = []
    far_values = []
    for step in range(depth, 0, -1):
        moved_key, moved_value = from_behind((key_norm, values), ("seq", "head"), step)
        far_keys.append(moved_key)
        far_values.append(moved_value)
    key_ext = jnp.concatenate(far_keys + [key_norm], 0)
    value_ext = jnp.concatenate(far_values + [values], 0)
    starts = clip_start(clip_lengths, first + jnp.arange(count, dtype=jnp.int32))
    attended, query_low, key_acc, value_acc = attend(
        query_norm.reshape(count, heads, HD),
        spread_heads(key_ext, kv_heads, repeat),
        spread_heads(value_ext, kv_heads, repeat),
        out_grad.reshape(count, heads, HD),
        first,
        starts,
        min(row_block, count),
    )
    key_acc = fold_heads(key_acc, kv_heads, repeat)
    value_acc = fold_heads(value_acc, kv_heads, repeat)
    front_key = key_acc[:MOST]
    front_value = value_acc[:MOST]
    key_total = key_acc[MOST:]
    value_total = value_acc[MOST:]
    for step in range(depth, 0, -1):
        begin = (depth - step) * count
        back_key, back_value = (
            from_behind(
                front_key[begin : begin + count].astype(jnp.bfloat16), ("seq", "head"), -step
            ).astype(jnp.float32),
            from_behind(
                front_value[begin : begin + count].astype(jnp.bfloat16), ("seq", "head"), -step
            ).astype(jnp.float32),
        )
        key_total = key_total + back_key
        value_total = value_total + back_value
    attended = attended.reshape(count, width)
    query_low = query_low.reshape(count, width)
    key_low = key_total.reshape(count, kv_heads * HD).astype(jnp.bfloat16)
    value_grad = value_total.reshape(count, kv_heads * HD).astype(jnp.bfloat16)
    query_grad, query_gain = unnormalize(
        query_low, query_unit, query_factor, query_gain_rows, modality
    )
    key_grad, key_gain = unnormalize(key_low, key_unit, key_factor, key_gain_rows, modality)
    query_gain_grad, key_gain_grad = lax.psum((query_gain, key_gain), ("seq", "head"))
    return (attended, query_grad, key_grad, value_grad, query_gain_grad, key_gain_grad)


def solution(mesh):
    return jax.shard_map(
        on_device,
        mesh=mesh,
        in_specs=(
            P(("seq", "head"), None),
            P(("seq", "head"), None),
            P(("seq", "head"), None),
            P(("seq", "head")),
            P(),
            P(),
            P(),
            P(("seq", "head"), None),
        ),
        out_specs=(
            P(("seq", "head"), None),
            P(("seq", "head"), None),
            P(("seq", "head"), None),
            P(("seq", "head"), None),
            P(),
            P(),
        ),
        check_vma=False,
    )
```

```python
import functools
import math

import jax
import jax.numpy as jnp
from jax import lax
from jax.experimental import pallas as pl
from jax.experimental.pallas import tpu as pltpu
from jax.sharding import PartitionSpec as P

HD = 128
MOST = 512
EPS = 1e-06
AXES = ("seq", "head")
CHUNKS = 2
SLAB = 2
FAR = -1e30


def shifted(value, steps):
    count = lax.axis_size(AXES)
    first, last = (max(0, -steps), min(count, count - steps))
    return lax.ppermute(value, AXES, [(source, source + steps) for source in range(first, last)])


def clip_start(clip_lengths, positions):
    order = jnp.arange(clip_lengths.shape[0], dtype=jnp.int32)
    begins = jnp.sum(jnp.where(order[None, :] < order[:, None], clip_lengths[None, :], 0), axis=1)
    chosen = jnp.where(
        begins[None, :] <= positions[:, None], begins[None, :], jnp.zeros((), jnp.int32)
    )
    return jnp.max(chosen, axis=1)


def nn(a, b):
    return lax.dot_general(a, b, (((1,), (0,)), ((), ())), preferred_element_type=jnp.float32)


def nt(a, b):
    return lax.dot_general(a, b, (((1,), (1,)), ((), ())), preferred_element_type=jnp.float32)


def modality_sums(picks, terms):
    return lax.dot_general(
        picks,
        terms,
        (((1,), (1,)), ((), ())),
        precision=lax.Precision.HIGHEST,
        preferred_element_type=jnp.float32,
    )


def attend_kernel(depth, repeat, aliased, *refs):
    blocks = depth + 1
    starts, mod_row, queries, grads, query_gain, key_gain = refs[:6]
    key_refs = refs[6 : 6 + blocks]
    value_refs = refs[6 + blocks : 6 + 2 * blocks]
    mod_refs = refs[6 + 2 * blocks : 6 + 3 * blocks]
    rest = refs[6 + 3 * blocks + (2 if aliased else 0) :]
    attended, query_back = rest[:2]
    back_refs = rest[2 : 2 + blocks]
    query_sums, key_sums, bias = rest[2 + blocks :]
    rows = queries.shape[0]
    span = blocks * rows
    scale = 1.0 / math.sqrt(HD)
    width = SLAB * HD

    @pl.when(pl.program_id(0) == 0)
    def _():
        key_at = lax.broadcasted_iota(jnp.int32, (span, rows), 0)
        query_at = lax.broadcasted_iota(jnp.int32, (span, rows), 1) + depth * rows
        allowed = (key_at >= starts[...]) & (key_at <= query_at)
        bias[...] = jnp.where(allowed, 0.0, FAR)

    key_raw = jnp.concatenate([r[...] for r in key_refs], 0).astype(jnp.float32)
    key_factor = lax.rsqrt(jnp.mean(key_raw * key_raw, axis=1, keepdims=True) + EPS)
    key_unit = key_raw * key_factor
    key_mod = jnp.concatenate([r[...] for r in mod_refs], 0).astype(jnp.float32) > 0.5
    key_norm = (key_unit * jnp.where(key_mod, key_gain[1:2, :], key_gain[0:1, :])).astype(
        jnp.bfloat16
    )
    value = jnp.concatenate([r[...] for r in value_refs], 0)
    key_turned = key_norm.T
    value_turned = value.T
    motion = mod_row[...] == 1
    kinds = lax.broadcasted_iota(jnp.int32, (8, rows), 0)
    picks = (kinds == mod_row[...]).astype(jnp.float32)

    key_acc = None
    value_acc = None
    for slab in range(repeat // SLAB):
        heads = [slab * SLAB + n for n in range(SLAB)]

        def turned(ref):
            return jnp.concatenate(
                [ref[:, h * HD : (h + 1) * HD].astype(jnp.float32).T for h in heads], 1
            )

        raw = turned(queries)
        grad = turned(grads)
        grad_low = grad.astype(jnp.bfloat16)
        factor = lax.rsqrt(jnp.mean(raw * raw, axis=0, keepdims=True) + EPS)
        unit = raw * factor
        gain = jnp.concatenate(
            [
                jnp.where(
                    motion,
                    query_gain[h * HD : (h + 1) * HD, 1:2],
                    query_gain[h * HD : (h + 1) * HD, 0:1],
                )
                for h in heads
            ],
            1,
        )
        query_norm = (unit * gain).astype(jnp.bfloat16)
        shield = jnp.concatenate([bias[...]] * SLAB, 1)
        scores = nn(key_norm, query_norm) * (scale * math.log2(math.e)) + shield
        expo = jnp.exp2(scores - jnp.max(scores, axis=0, keepdims=True))
        probs = expo * (1.0 / jnp.sum(expo, axis=0, keepdims=True))
        probs_low = probs.astype(jnp.bfloat16)
        seen = nn(value_turned, probs_low).astype(jnp.bfloat16)
        seen_wide = seen.astype(jnp.float32)
        delta = jnp.sum(grad * seen_wide, axis=0, keepdims=True)
        prob_grad = nn(value, grad_low)
        score_grad = (probs * (prob_grad - delta) * scale).astype(jnp.bfloat16)
        low = nn(key_turned, score_grad).astype(jnp.bfloat16).astype(jnp.float32)
        along = low * gain
        back = factor * (along - unit * jnp.mean(along * unit, axis=0, keepdims=True))
        term = low * unit
        for n, h in enumerate(heads):
            part = slice(n * HD, (n + 1) * HD)
            cols = slice(h * HD, (h + 1) * HD)
            attended[:, cols] = seen_wide[:, part].T.astype(jnp.bfloat16)
            query_back[:, cols] = back[:, part].T.astype(jnp.bfloat16)
            query_sums[:, cols] = modality_sums(picks, term[:, part])
        key_step = nt(score_grad, query_norm)
        value_step = nt(probs_low, grad_low)
        key_acc = key_step if key_acc is None else key_acc + key_step
        value_acc = value_step if value_acc is None else value_acc + value_step

    for n, ref in enumerate(back_refs):
        part = slice(n * rows, (n + 1) * rows)
        ref[:, :HD] = key_acc[part].astype(ref.dtype)
        ref[:, HD:] = value_acc[part].astype(ref.dtype)
    term = key_acc * key_unit
    of_motion = jnp.sum(jnp.where(key_mod, term, 0.0), axis=0, keepdims=True)
    of_text = jnp.sum(jnp.where(key_mod, 0.0, term), axis=0, keepdims=True)
    lines = lax.broadcasted_iota(jnp.int32, (8, HD), 0)
    key_sums[...] = jnp.where(lines == 0, of_text, jnp.where(lines == 1, of_motion, 0.0))


def attend(first_head, kv, starts, mod_row, queries, grads, query_gain, key_gain, held, mods, before):
    rows, width = queries.shape
    repeat = width // HD // (key_gain.shape[1] // HD)
    blocks = len(held)
    group = repeat * HD

    def at(shape, index):
        return pl.BlockSpec(shape, index)

    whole = lambda g: (0, 0)
    here = lambda g: (0, first_head + g)
    in_specs = [
        at((1, rows), whole),
        at((1, rows), whole),
        at((rows, group), here),
        at((rows, group), here),
        at((group, 2), lambda g: (first_head + g, 0)),
        at((2, HD), here),
    ]
    in_specs += [at((rows, HD), lambda g: (0, g))] * blocks
    in_specs += [at((rows, HD), lambda g: (0, kv + g))] * blocks
    in_specs += [at((rows, HD), lambda g, lane=mods[1]: (0, lane))] * blocks
    operands = [starts, mod_row, queries, grads, query_gain, key_gain, *held, *held, *mods[0]]
    aliases = {}
    if before is not None:
        aliases = {len(operands): 0, len(operands) + 1: 1}
        operands += list(before)
        in_specs += [pl.BlockSpec(memory_space=pl.ANY)] * 2
    big = jax.ShapeDtypeStruct((rows, width), jnp.bfloat16)
    pair = lambda dtype: jax.ShapeDtypeStruct((rows, kv * 2 * HD), dtype)
    outs = [big, big, pair(jnp.bfloat16)] + [pair(jnp.float32)] * (blocks - 1)
    outs += [
        jax.ShapeDtypeStruct((8, kv * group), jnp.float32),
        jax.ShapeDtypeStruct((8, kv * HD), jnp.float32),
    ]
    out_specs = [at((rows, group), here)] * 2
    out_specs += [at((rows, 2 * HD), lambda g: (0, g))] * blocks
    out_specs += [at((8, group), lambda g: (0, g)), at((8, HD), lambda g: (0, g))]
    return pl.pallas_call(
        functools.partial(attend_kernel, blocks - 1, repeat, before is not None),
        grid=(kv,),
        in_specs=in_specs,
        out_specs=out_specs,
        out_shape=outs,
        scratch_shapes=[pltpu.VMEM((blocks * rows, rows), jnp.float32)],
        input_output_aliases=aliases,
        compiler_params=pltpu.CompilerParams(vmem_limit_bytes=40 * 1024 * 1024),
        cost_estimate=pl.CostEstimate(
            flops=kv * repeat * 12 * rows * blocks * rows * HD,
            bytes_accessed=kv * group * rows * 8 + blocks * rows * kv * HD * 12,
            transcendentals=kv * repeat * rows * blocks * rows,
        ),
        name="attend",
    )(*operands)


def finish_kernel(arrived, own, keys, mod, key_gain, key_back, value_back):
    total = arrived[...].astype(jnp.float32) + own[...]
    low = total[:, :HD].astype(jnp.bfloat16).astype(jnp.float32)
    raw = keys[...].astype(jnp.float32)
    factor = lax.rsqrt(jnp.mean(raw * raw, axis=1, keepdims=True) + EPS)
    unit = raw * factor
    gain = jnp.where(mod[...].astype(jnp.float32) > 0.5, key_gain[1:2, :], key_gain[0:1, :])
    along = low * gain
    back = factor * (along - unit * jnp.mean(along * unit, axis=1, keepdims=True))
    key_back[...] = back.astype(jnp.bfloat16)
    value_back[...] = total[:, HD:].astype(jnp.bfloat16)


def finish(first_head, kv, arrived, own, keys, mods, key_gain):
    rows = keys.shape[0]
    here = lambda g: (0, first_head + g)
    low = jax.ShapeDtypeStruct((rows, kv * HD), jnp.bfloat16)
    return pl.pallas_call(
        finish_kernel,
        grid=(kv,),
        in_specs=[
            pl.BlockSpec((rows, 2 * HD), lambda g: (0, g)),
            pl.BlockSpec((rows, 2 * HD), lambda g: (0, g)),
            pl.BlockSpec((rows, HD), here),
            pl.BlockSpec((rows, HD), lambda g: (0, mods[1])),
            pl.BlockSpec((2, HD), here),
        ],
        out_specs=[pl.BlockSpec((rows, HD), lambda g: (0, g))] * 2,
        out_shape=[low, low],
        name="finish",
    )(arrived, own, keys, mods[0][-1], key_gain)


def summed(value):
    count = lax.axis_size(AXES)
    bit = 1
    while bit < count:
        value = value + lax.ppermute(value, AXES, [(i, i ^ bit) for i in range(count)])
        bit *= 2
    return value


def on_device(queries, keys, values, modality, clip_lengths, query_gains, key_gains, out_grad):
    count, width = queries.shape
    kv_heads = keys.shape[1] // HD
    kv = kv_heads // CHUNKS
    depth = (MOST + count - 1) // count
    first = lax.axis_index(AXES) * count
    mod_lanes = jnp.broadcast_to(modality.astype(jnp.bfloat16)[:, None], (count, HD))
    held = []
    for chunk in range(CHUNKS):
        part = slice(chunk * kv * HD, (chunk + 1) * kv * HD)
        block = [keys[:, part], values[:, part]] + ([mod_lanes] if chunk == 0 else [])
        held.append([jnp.concatenate(block, 1)])
    for chunk in range(CHUNKS):
        for _ in range(depth):
            held[chunk].append(shifted(held[chunk][-1], 1))
    held = [blocks[::-1] for blocks in held]
    mods = (held[0], 2 * kv)

    starts = clip_start(clip_lengths, first + jnp.arange(count, dtype=jnp.int32))
    starts = (starts - first + depth * count)[None, :]
    mod_row = modality[None, :]
    gain_columns = query_gains.T
    before = None
    sums = []
    key_parts = []
    value_parts = []
    rings = []
    for chunk in range(CHUNKS):
        outs = attend(
            chunk * kv,
            kv,
            starts,
            mod_row,
            queries,
            out_grad,
            gain_columns,
            key_gains,
            held[chunk],
            mods,
            before,
        )
        before = outs[:2]
        sums.append(outs[-2:])
        rings.append(outs[2:-2])
    for chunk in range(CHUNKS):
        backs = rings[chunk]
        moving = backs[0]
        for n in range(1, depth + 1):
            moving = shifted(moving, -1)
            if n < depth:
                moving = (moving.astype(jnp.float32) + backs[n]).astype(jnp.bfloat16)
        key_part, value_part = finish(
            chunk * kv, kv, moving, backs[depth], keys, mods, key_gains
        )
        key_parts.append(key_part)
        value_parts.append(value_part)
    attended, query_grad = before
    gains = jnp.concatenate([q[:2] for q, _ in sums] + [k[:2] for _, k in sums], 1)
    gains = summed(gains.reshape(-1, HD)).reshape(2, -1)
    return (
        attended,
        query_grad,
        jnp.concatenate(key_parts, 1),
        jnp.concatenate(value_parts, 1),
        gains[:, :width],
        gains[:, width:],
    )


def solution(mesh):
    rows = P(AXES, None)
    return jax.shard_map(
        on_device,
        mesh=mesh,
        in_specs=(rows, rows, rows, P(AXES), P(), P(), P(), rows),
        out_specs=(rows, rows, rows, rows, P(), P()),
        check_vma=False,
    )
```

```python
import functools
import math

import jax
import jax.numpy as jnp
from jax import lax
from jax.experimental import pallas as pl
from jax.experimental.pallas import tpu as pltpu
from jax.sharding import PartitionSpec as P

HD = 128
MOST = 512
EPS = 1e-06
AXES = ("seq", "head")
CHUNKS = 2
NEAR = 3
TURNS = (2, 2, 2, 2)
TIED = True
VMEM = 62 * 1024 * 1024
COST = 1
SLAB = 4
FAR = -1e30


def shifted(value, steps):
    count = lax.axis_size(AXES)
    first, last = (max(0, -steps), min(count, count - steps))
    return lax.ppermute(value, AXES, [(source, source + steps) for source in range(first, last)])


def clip_start(clip_lengths, positions):
    order = jnp.arange(clip_lengths.shape[0], dtype=jnp.int32)
    begins = jnp.sum(jnp.where(order[None, :] < order[:, None], clip_lengths[None, :], 0), axis=1)
    chosen = jnp.where(
        begins[None, :] <= positions[:, None], begins[None, :], jnp.zeros((), jnp.int32)
    )
    return jnp.max(chosen, axis=1)


def nn(a, b):
    return lax.dot_general(a, b, (((1,), (0,)), ((), ())), preferred_element_type=jnp.float32)


def nt(a, b):
    return lax.dot_general(a, b, (((1,), (1,)), ((), ())), preferred_element_type=jnp.float32)


def modality_sums(picks, terms):
    return lax.dot_general(
        picks,
        terms,
        (((1,), (1,)), ((), ())),
        precision=lax.Precision.HIGHEST,
        preferred_element_type=jnp.float32,
    )


def attend_kernel(depth, repeat, skip, *refs):
    blocks = depth + 1
    starts, mod_row, queries, grads, query_gain, key_gain = refs[:6]
    key_refs = refs[6 : 6 + blocks]
    value_refs = refs[6 + blocks : 6 + 2 * blocks]
    mod_refs = refs[6 + 2 * blocks : 6 + 3 * blocks]
    rest = refs[6 + 3 * blocks + skip :]
    attended, query_back = rest[:2]
    back_refs = rest[2 : 2 + blocks]
    query_sums, key_sums, bias = rest[2 + blocks :]
    rows = queries.shape[0]
    span = blocks * rows
    scale = 1.0 / math.sqrt(HD)
    width = SLAB * HD

    @pl.when(pl.program_id(0) == 0)
    def _():
        key_at = lax.broadcasted_iota(jnp.int32, (span, rows), 0)
        query_at = lax.broadcasted_iota(jnp.int32, (span, rows), 1) + depth * rows
        allowed = (key_at >= starts[...]) & (key_at <= query_at)
        bias[...] = jnp.where(allowed, 0.0, FAR)

    key_raw = jnp.concatenate([r[...] for r in key_refs], 0).astype(jnp.float32)
    key_factor = lax.rsqrt(jnp.mean(key_raw * key_raw, axis=1, keepdims=True) + EPS)
    key_unit = key_raw * key_factor
    key_mod = jnp.concatenate([r[...] for r in mod_refs], 0).astype(jnp.float32) > 0.5
    key_norm = (key_unit * jnp.where(key_mod, key_gain[1:2, :], key_gain[0:1, :])).astype(
        jnp.bfloat16
    )
    value = jnp.concatenate([r[...] for r in value_refs], 0)
    key_turned = key_norm.T
    value_turned = value.T
    motion = mod_row[...] == 1
    kinds = lax.broadcasted_iota(jnp.int32, (8, rows), 0)
    picks = (kinds == mod_row[...]).astype(jnp.float32)

    key_acc = None
    value_acc = None
    for slab in range(repeat // SLAB):
        heads = [slab * SLAB + n for n in range(SLAB)]

        def turned(ref):
            return jnp.concatenate(
                [ref[:, h * HD : (h + 1) * HD].astype(jnp.float32).T for h in heads], 1
            )

        raw = turned(queries)
        grad = turned(grads)
        grad_low = grad.astype(jnp.bfloat16)
        factor = lax.rsqrt(jnp.mean(raw * raw, axis=0, keepdims=True) + EPS)
        unit = raw * factor
        gain = jnp.concatenate(
            [
                jnp.where(
                    motion,
                    query_gain[h * HD : (h + 1) * HD, 1:2],
                    query_gain[h * HD : (h + 1) * HD, 0:1],
                )
                for h in heads
            ],
            1,
        )
        query_norm = (unit * gain).astype(jnp.bfloat16)
        shield = jnp.concatenate([bias[...]] * SLAB, 1)
        scores = nn(key_norm, query_norm) * (scale * math.log2(math.e)) + shield
        expo = jnp.exp2(scores - jnp.max(scores, axis=0, keepdims=True))
        probs = expo * (1.0 / jnp.sum(expo, axis=0, keepdims=True))
        probs_low = probs.astype(jnp.bfloat16)
        seen = nn(value_turned, probs_low).astype(jnp.bfloat16)
        seen_wide = seen.astype(jnp.float32)
        delta = jnp.sum(grad * seen_wide, axis=0, keepdims=True)
        prob_grad = nn(value, grad_low)
        score_grad = (probs * (prob_grad - delta) * scale).astype(jnp.bfloat16)
        low = nn(key_turned, score_grad).astype(jnp.bfloat16).astype(jnp.float32)
        along = low * gain
        back = factor * (along - unit * jnp.mean(along * unit, axis=0, keepdims=True))
        term = low * unit
        for n, h in enumerate(heads):
            part = slice(n * HD, (n + 1) * HD)
            cols = slice(h * HD, (h + 1) * HD)
            attended[:, cols] = seen_wide[:, part].T.astype(jnp.bfloat16)
            query_back[:, cols] = back[:, part].T.astype(jnp.bfloat16)
            query_sums[:, cols] = modality_sums(picks, term[:, part])
        key_step = nt(score_grad, query_norm)
        value_step = nt(probs_low, grad_low)
        key_acc = key_step if key_acc is None else key_acc + key_step
        value_acc = value_step if value_acc is None else value_acc + value_step

    for n, ref in enumerate(back_refs):
        part = slice(n * rows, (n + 1) * rows)
        ref[:, :HD] = key_acc[part].astype(ref.dtype)
        ref[:, HD:] = value_acc[part].astype(ref.dtype)
    term = key_acc * key_unit
    of_motion = jnp.sum(jnp.where(key_mod, term, 0.0), axis=0, keepdims=True)
    of_text = jnp.sum(jnp.where(key_mod, 0.0, term), axis=0, keepdims=True)
    lines = lax.broadcasted_iota(jnp.int32, (8, HD), 0)
    key_sums[...] = jnp.where(lines == 0, of_text, jnp.where(lines == 1, of_motion, 0.0))


def attend(first_head, kv, chunk, starts, mod_row, queries, grads, query_gain, key_gain, held, mods, before, token):
    start_head, chunk_kv = chunk
    rows, width = queries.shape
    repeat = width // HD // (key_gain.shape[1] // HD)
    blocks = len(held)
    group = repeat * HD

    def at(shape, index):
        return pl.BlockSpec(shape, index)

    whole = lambda g: (0, 0)
    here = lambda g: (0, start_head + first_head + g)
    local = lambda g: (0, first_head + g)
    in_specs = [
        at((1, rows), whole),
        at((1, rows), whole),
        at((rows, group), here),
        at((rows, group), here),
        at((group, 2), lambda g: (start_head + first_head + g, 0)),
        at((2, HD), here),
    ]
    in_specs += [at((rows, HD), local)] * blocks
    in_specs += [at((rows, HD), lambda g: (0, chunk_kv + first_head + g))] * blocks
    in_specs += [at((rows, HD), lambda g, lane=mods[1]: (0, lane))] * blocks
    operands = [starts, mod_row, queries, grads, query_gain, key_gain, *held, *held, *mods[0]]
    aliases = {}
    extra = [(n, x) for n, x in enumerate(before) if x is not None]
    for n, x in extra:
        aliases[len(operands)] = n
        operands.append(x)
    if token is not None:
        operands.append(token)
    in_specs += [pl.BlockSpec(memory_space=pl.ANY)] * (len(operands) - len(in_specs))
    skip = len(operands) - 6 - 3 * blocks
    big = jax.ShapeDtypeStruct((rows, width), jnp.bfloat16)
    pair = lambda dtype: jax.ShapeDtypeStruct((rows, chunk_kv * 2 * HD), dtype)
    outs = [big, big, pair(jnp.bfloat16)] + [pair(jnp.float32)] * (blocks - 1)
    outs += [
        jax.ShapeDtypeStruct((8, chunk_kv * group), jnp.float32),
        jax.ShapeDtypeStruct((8, chunk_kv * HD), jnp.float32),
    ]
    out_specs = [at((rows, group), here)] * 2
    out_specs += [at((rows, 2 * HD), local)] * blocks
    out_specs += [at((8, group), local), at((8, HD), local)]
    return pl.pallas_call(
        functools.partial(attend_kernel, blocks - 1, repeat, skip),
        grid=(kv,),
        in_specs=in_specs,
        out_specs=out_specs,
        out_shape=outs,
        scratch_shapes=[pltpu.VMEM((blocks * rows, rows), jnp.float32)],
        input_output_aliases=aliases,
        compiler_params=pltpu.CompilerParams(vmem_limit_bytes=VMEM),
        cost_estimate=pl.CostEstimate(
            flops=COST * kv * repeat * 12 * rows * blocks * rows * HD,
            bytes_accessed=kv * group * rows * 8 + blocks * rows * kv * HD * 12,
            transcendentals=kv * repeat * rows * blocks * rows,
        ),
        name="attend",
    )(*operands)


def finish_kernel(*refs):
    pairs, (keys, mod, key_gain, key_back, value_back) = refs[: 2 * CHUNKS], refs[2 * CHUNKS :]
    motion = mod[...].astype(jnp.float32) > 0.5
    kv = keys.shape[1] // HD // CHUNKS
    for g in range(CHUNKS * kv):
        arrived, own = pairs[2 * (g // kv) : 2 * (g // kv) + 2]
        cols = slice(g * HD, (g + 1) * HD)
        at = 2 * (g % kv) * HD
        both = arrived[:, at : at + 2 * HD].astype(jnp.float32) + own[:, at : at + 2 * HD]
        low = both[:, :HD].astype(jnp.bfloat16).astype(jnp.float32)
        raw = keys[:, cols].astype(jnp.float32)
        factor = lax.rsqrt(jnp.mean(raw * raw, axis=1, keepdims=True) + EPS)
        unit = raw * factor
        along = low * jnp.where(motion, key_gain[1:2, cols], key_gain[0:1, cols])
        back = factor * (along - unit * jnp.mean(along * unit, axis=1, keepdims=True))
        key_back[:, cols] = back.astype(jnp.bfloat16)
        value_back[:, cols] = both[:, HD:].astype(jnp.bfloat16)


def finish(pairs, keys, mods, key_gain):
    low = jax.ShapeDtypeStruct(keys.shape, jnp.bfloat16)
    full = lambda x: pl.BlockSpec(x.shape, lambda g: (0, 0))
    operands = [x for pair in pairs for x in pair] + [keys]
    return pl.pallas_call(
        finish_kernel,
        grid=(1,),
        in_specs=[full(x) for x in operands]
        + [pl.BlockSpec((keys.shape[0], HD), lambda g: (0, mods[1])), full(key_gain)],
        out_specs=[full(keys)] * 2,
        out_shape=[low, low],
        compiler_params=pltpu.CompilerParams(vmem_limit_bytes=VMEM),
        name="finish",
    )(*operands, mods[0][-1], key_gain)


def after(value, *others):
    return lax.optimization_barrier((value, *others))[0]


def on_device(queries, keys, values, modality, clip_lengths, query_gains, key_gains, out_grad):
    count, width = queries.shape
    devices = lax.axis_size(AXES)
    kv_heads = keys.shape[1] // HD
    kv = kv_heads // CHUNKS
    depth = (MOST + count - 1) // count
    first = lax.axis_index(AXES) * count
    mod_lanes = jnp.broadcast_to(modality.astype(jnp.bfloat16)[:, None], (count, HD))
    low_part = slice(0, kv * HD)
    high_part = slice(kv * HD, 2 * kv * HD)
    ahead = [jnp.concatenate([keys[:, low_part], values[:, low_part], mod_lanes], 1)]
    behind = [jnp.concatenate([keys[:, high_part], values[:, high_part]], 1)]
    for n in range(depth):
        ahead.append(shifted(ahead[-1], 1))
        behind.append(shifted(behind[-1], 1))
    mods = (ahead[::-1], 2 * kv)

    starts = clip_start(clip_lengths, first + jnp.arange(count, dtype=jnp.int32))
    starts = (starts - first + depth * count)[None, :]
    mod_row = modality[None, :]
    gain_columns = query_gains.T
    outputs = depth + 5

    def attended_chunk(chunk, held, large, sizes, tokens):
        outs = [*large] + [None] * (outputs - 2)
        head = 0
        for size, token in zip(sizes, tokens):
            outs = attend(
                head,
                size,
                (chunk * kv, kv),
                starts,
                mod_row,
                queries,
                out_grad,
                gain_columns,
                key_gains,
                held[::-1],
                mods,
                outs,
                token(),
            )
            head += size
            yield outs

    def add(arrived, part):
        return (arrived.astype(jnp.float32) + part).astype(jnp.bfloat16)

    (one,) = attended_chunk(0, ahead, [None, None], [kv], [lambda: None])
    (two,) = attended_chunk(1, behind, one[:2], [kv], [lambda: None])
    backs = (one[2:-2], two[2:-2])
    attended, query_grad = two[:2]
    gains = jnp.concatenate([one[-2][:2], two[-2][:2], one[-1][:2], two[-1][:2]], 1).reshape(-1, HD)
    bits = [1 << n for n in range(devices.bit_length() - 1)]
    bits = bits[NEAR:] + bits[:NEAR]
    done = 0
    moved = [shifted(part[0], -1) for part in backs]
    for n in range(1, depth + 1):
        for bit in bits[done : done + TURNS[n - 1]]:
            gains = gains + lax.ppermute(gains, AXES, [(i, i ^ bit) for i in range(devices)])
        done += TURNS[n - 1]
        if n < depth:
            sent = [add(arrived, part[n]) for arrived, part in zip(moved, backs)]
            if TIED:
                gains = after(gains, sent[0])
                sent[1] = after(sent[1], gains)
            moved = [shifted(x, -1) for x in sent]
    if TURNS == (0, 0, 0, 0):
        gains = after(gains, *moved)
        for bit in bits:
            gains = gains + lax.ppermute(gains, AXES, [(i, i ^ bit) for i in range(devices)])
    key_grad, value_grad = finish(
        [(arrived, part[depth]) for arrived, part in zip(moved, backs)], keys, mods, key_gains
    )
    gains = gains.reshape(2, -1)
    return attended, query_grad, key_grad, value_grad, gains[:, :width], gains[:, width:]


def solution(mesh):
    rows = P(AXES, None)
    return jax.shard_map(
        on_device,
        mesh=mesh,
        in_specs=(rows, rows, rows, P(AXES), P(), P(), P(), rows),
        out_specs=(rows, rows, rows, rows, P(), P()),
        check_vma=False,
    )
```

```python
import functools
import math

import jax
import jax.numpy as jnp
from jax import lax
from jax.experimental import pallas as pl
from jax.experimental.pallas import tpu as pltpu
from jax.sharding import PartitionSpec as P

HD = 128
MOST = 512
EPS = 1e-06
AXES = ("seq", "head")
CHUNKS = 2
NEAR = 3
TURNS = (2, 2, 2, 2)
RINGS = 2
VMEM = 62 * 1024 * 1024
COST = 1
SLAB = 4
FAR = -1e30


def shifted(value, steps):
    count = lax.axis_size(AXES)
    first, last = (max(0, -steps), min(count, count - steps))
    return lax.ppermute(value, AXES, [(source, source + steps) for source in range(first, last)])


def clip_start(clip_lengths, positions):
    order = jnp.arange(clip_lengths.shape[0], dtype=jnp.int32)
    begins = jnp.sum(jnp.where(order[None, :] < order[:, None], clip_lengths[None, :], 0), axis=1)
    chosen = jnp.where(
        begins[None, :] <= positions[:, None], begins[None, :], jnp.zeros((), jnp.int32)
    )
    return jnp.max(chosen, axis=1)


def nn(a, b):
    return lax.dot_general(a, b, (((1,), (0,)), ((), ())), preferred_element_type=jnp.float32)


def nt(a, b):
    return lax.dot_general(a, b, (((1,), (1,)), ((), ())), preferred_element_type=jnp.float32)


def attend_kernel(depth, repeat, skip, *refs):
    blocks = depth + 1
    starts, mod_row, queries, grads, query_gain, key_gain = refs[:6]
    key_refs = refs[6 : 6 + blocks]
    value_refs = refs[6 + blocks : 6 + 2 * blocks]
    mod_refs = refs[6 + 2 * blocks : 6 + 3 * blocks]
    rest = refs[6 + 3 * blocks + skip :]
    attended, query_back = rest[:2]
    back_refs = rest[2 : 2 + blocks]
    sums, bias, kinds = rest[2 + blocks :]
    rows = queries.shape[0]
    span = blocks * rows
    scale = 1.0 / math.sqrt(HD)
    width = SLAB * HD

    @pl.when(pl.program_id(0) == 0)
    def _():
        key_at = lax.broadcasted_iota(jnp.int32, (span, rows), 0)
        query_at = lax.broadcasted_iota(jnp.int32, (span, rows), 1) + depth * rows
        allowed = (key_at >= starts[...]) & (key_at <= query_at)
        bias[...] = jnp.where(allowed, 0.0, FAR)
        for n, ref in enumerate(mod_refs):
            row = ref[...].astype(jnp.float32)[0:1, :]
            kinds[n * rows : (n + 1) * rows, :] = jnp.broadcast_to(row, (HD, rows)).T

    key_raw = jnp.concatenate([r[...] for r in key_refs], 0).astype(jnp.float32)
    key_factor = lax.rsqrt(jnp.mean(key_raw * key_raw, axis=1, keepdims=True) + EPS)
    key_unit = key_raw * key_factor
    key_mod = kinds[...] > 0.5
    own_mod = kinds[depth * rows :, :] > 0.5
    key_norm = (key_unit * jnp.where(key_mod, key_gain[1:2, :], key_gain[0:1, :])).astype(
        jnp.bfloat16
    )
    value = jnp.concatenate([r[...] for r in value_refs], 0)
    key_turned = key_norm.T
    value_turned = value.T
    motion = mod_row[...] == 1

    sums[8:16, :] = jnp.zeros((8, HD), jnp.float32)
    key_acc = None
    value_acc = None
    for slab in range(repeat // SLAB):
        heads = [slab * SLAB + n for n in range(SLAB)]

        def turned(ref):
            return jnp.concatenate(
                [ref[:, h * HD : (h + 1) * HD].astype(jnp.float32).T for h in heads], 1
            )

        raw = turned(queries)
        grad = turned(grads)
        grad_low = grad.astype(jnp.bfloat16)
        factor = lax.rsqrt(jnp.mean(raw * raw, axis=0, keepdims=True) + EPS)
        unit = raw * factor
        gain = jnp.concatenate(
            [
                jnp.where(
                    motion,
                    query_gain[h * HD : (h + 1) * HD, 1:2],
                    query_gain[h * HD : (h + 1) * HD, 0:1],
                )
                for h in heads
            ],
            1,
        )
        query_norm = (unit * gain).astype(jnp.bfloat16)
        shield = jnp.concatenate([bias[...]] * SLAB, 1)
        scores = nn(key_norm, query_norm) * (scale * math.log2(math.e)) + shield
        expo = jnp.exp2(scores - jnp.max(scores, axis=0, keepdims=True))
        probs = expo * (1.0 / jnp.sum(expo, axis=0, keepdims=True))
        probs_low = probs.astype(jnp.bfloat16)
        seen = nn(value_turned, probs_low).astype(jnp.bfloat16)
        seen_wide = seen.astype(jnp.float32)
        delta = jnp.sum(grad * seen_wide, axis=0, keepdims=True)
        prob_grad = nn(value, grad_low)
        score_grad = (probs * (prob_grad - delta) * scale).astype(jnp.bfloat16)
        low = nn(key_turned, score_grad).astype(jnp.bfloat16).astype(jnp.float32)
        along = low * gain
        back = factor * (along - unit * jnp.mean(along * unit, axis=0, keepdims=True))
        term = low * unit
        for n, h in enumerate(heads):
            part = slice(n * HD, (n + 1) * HD)
            cols = slice(h * HD, (h + 1) * HD)
            attended[:, cols] = seen_wide[:, part].T.astype(jnp.bfloat16)
            query_back[:, cols] = back[:, part].T.astype(jnp.bfloat16)
            turn = term[:, part].T
            sums[2 * h : 2 * h + 1, :] = jnp.sum(jnp.where(own_mod, 0.0, turn), axis=0, keepdims=True)
            sums[2 * h + 1 : 2 * h + 2, :] = jnp.sum(jnp.where(own_mod, turn, 0.0), axis=0, keepdims=True)
        key_step = nt(score_grad, query_norm)
        value_step = nt(probs_low, grad_low)
        key_acc = key_step if key_acc is None else key_acc + key_step
        value_acc = value_step if value_acc is None else value_acc + value_step

    for n, ref in enumerate(back_refs):
        part = slice(n * rows, (n + 1) * rows)
        ref[:, :HD] = key_acc[part].astype(ref.dtype)
        ref[:, HD:] = value_acc[part].astype(ref.dtype)
    term = key_acc * key_unit
    of_motion = jnp.sum(jnp.where(key_mod, term, 0.0), axis=0, keepdims=True)
    of_text = jnp.sum(jnp.where(key_mod, 0.0, term), axis=0, keepdims=True)
    sums[2 * repeat : 2 * repeat + 1, :] = of_text
    sums[2 * repeat + 1 : 2 * repeat + 2, :] = of_motion


def attend(first_head, chunk_kv, starts, mod_row, queries, grads, query_gain, key_gain, held, mods, before, wide):
    rows, width = queries.shape
    kv_heads = key_gain.shape[1] // HD
    repeat = width // HD // kv_heads
    blocks = len(held)
    group = repeat * HD

    def at(shape, index):
        return pl.BlockSpec(shape, index)

    whole = lambda g: (0, 0)
    here = lambda g: (0, first_head + g)
    down = lambda g: (first_head + g, 0)
    local = here if wide else lambda g: (0, g)
    mod_at = mods[0].shape[0] // 16 - 1
    in_specs = [
        at((1, rows), whole),
        at((1, rows), whole),
        at((rows, group), here),
        at((rows, group), here),
        at((group, 2), down),
        at((2, HD), here),
    ]
    in_specs += [at((rows, HD), lambda g: (g, 0))] * blocks
    in_specs += [at((rows, HD), lambda g: (chunk_kv + g, 0))] * blocks
    in_specs += [at((16, HD), lambda g: (mod_at, 0))] * blocks
    operands = [starts, mod_row, queries, grads, query_gain, key_gain, *held, *held, *mods]
    aliases = {}
    for n, x in enumerate(before):
        if x is not None:
            aliases[len(operands)] = n
            operands.append(x)
    in_specs += [pl.BlockSpec(memory_space=pl.ANY)] * len(aliases)
    big = jax.ShapeDtypeStruct((rows, width), jnp.bfloat16)
    pair = lambda dtype: jax.ShapeDtypeStruct((rows, (kv_heads if wide else chunk_kv) * 2 * HD), dtype)
    outs = [big, big, pair(jnp.bfloat16)] + [pair(jnp.float32)] * (blocks - 1)
    outs += [jax.ShapeDtypeStruct((kv_heads * 16, HD), jnp.float32)]
    out_specs = [at((rows, group), here)] * 2
    out_specs += [at((rows, 2 * HD), local)] * blocks
    out_specs += [at((16, HD), down)]
    return pl.pallas_call(
        functools.partial(attend_kernel, blocks - 1, repeat, len(aliases)),
        grid=(chunk_kv,),
        in_specs=in_specs,
        out_specs=out_specs,
        out_shape=outs,
        scratch_shapes=[
            pltpu.VMEM((blocks * rows, rows), jnp.float32),
            pltpu.VMEM((blocks * rows, HD), jnp.float32),
        ],
        input_output_aliases=aliases,
        compiler_params=pltpu.CompilerParams(vmem_limit_bytes=VMEM),
        cost_estimate=pl.CostEstimate(
            flops=COST * chunk_kv * repeat * 12 * rows * blocks * rows * HD,
            bytes_accessed=chunk_kv * group * rows * 8 + blocks * rows * chunk_kv * HD * 12,
            transcendentals=chunk_kv * repeat * rows * blocks * rows,
        ),
        name="attend",
    )(*operands)


def finish_kernel(*refs):
    pairs, (keys, mod, key_gain, key_back, value_back) = refs[:-5], refs[-5:]
    motion = mod[...].astype(jnp.float32) > 0.5
    kv_heads = keys.shape[1] // HD
    kv = kv_heads // (len(pairs) // 2)
    for g in range(kv_heads):
        arrived, own = pairs[2 * (g // kv) : 2 * (g // kv) + 2]
        cols = slice(g * HD, (g + 1) * HD)
        at = 2 * (g % kv) * HD
        both = arrived[:, at : at + 2 * HD].astype(jnp.float32) + own[:, at : at + 2 * HD]
        low = both[:, :HD].astype(jnp.bfloat16).astype(jnp.float32)
        raw = keys[:, cols].astype(jnp.float32)
        factor = lax.rsqrt(jnp.mean(raw * raw, axis=1, keepdims=True) + EPS)
        unit = raw * factor
        along = low * jnp.where(motion, key_gain[1:2, cols], key_gain[0:1, cols])
        back = factor * (along - unit * jnp.mean(along * unit, axis=1, keepdims=True))
        key_back[:, cols] = back.astype(jnp.bfloat16)
        value_back[:, cols] = both[:, HD:].astype(jnp.bfloat16)


def finish(pairs, keys, mod_lanes, key_gain):
    low = jax.ShapeDtypeStruct(keys.shape, jnp.bfloat16)
    full = lambda x: pl.BlockSpec(x.shape, lambda g: (0, 0))
    operands = [x for pair in pairs for x in pair] + [keys, mod_lanes, key_gain]
    return pl.pallas_call(
        finish_kernel,
        grid=(1,),
        in_specs=[full(x) for x in operands],
        out_specs=[full(keys)] * 2,
        out_shape=[low, low],
        compiler_params=pltpu.CompilerParams(vmem_limit_bytes=VMEM),
        name="finish",
    )(*operands)


def after(value, *others):
    return lax.optimization_barrier((value, *others))[0]


def on_device(queries, keys, values, modality, clip_lengths, query_gains, key_gains, out_grad):
    count, width = queries.shape
    devices = lax.axis_size(AXES)
    kv_heads = keys.shape[1] // HD
    kv = kv_heads // CHUNKS
    depth = (MOST + count - 1) // count
    first = lax.axis_index(AXES) * count
    mod_lanes = jnp.broadcast_to(modality.astype(jnp.bfloat16)[:, None], (count, HD))
    mod_rows = jnp.broadcast_to(modality.astype(jnp.bfloat16)[None, :], (16, count))

    def payload(chunk):
        heads = range(chunk * kv, (chunk + 1) * kv)
        blocks = [x[:, h * HD : (h + 1) * HD] for x in (keys, values) for h in heads]
        return jnp.concatenate(blocks + ([mod_rows] if chunk == 0 else []), 0)

    ahead = [payload(0)]
    behind = [payload(1)]
    for n in range(depth):
        ahead.append(shifted(ahead[-1], 1))
        behind.append(shifted(behind[-1], 1))
    mods = ahead[::-1]

    starts = clip_start(clip_lengths, first + jnp.arange(count, dtype=jnp.int32))
    starts = (starts - first + depth * count)[None, :]
    mod_row = modality[None, :]
    gain_columns = query_gains.T

    def add(arrived, part):
        return (arrived.astype(jnp.float32) + part).astype(jnp.bfloat16)

    outs = [None] * (depth + 4)
    backs = []
    for chunk, held in enumerate((ahead, behind)):
        if RINGS > 1:
            outs = [*outs[:2], *[None] * (depth + 1), outs[-1]]
        outs = attend(
            chunk * kv,
            kv,
            starts,
            mod_row,
            queries,
            out_grad,
            gain_columns,
            key_gains,
            held[::-1],
            mods,
            outs,
            RINGS == 1,
        )
        backs.append(outs[2:-1])
    backs = backs[-RINGS:]
    attended, query_grad = outs[:2]
    gains = outs[-1]
    bits = [1 << n for n in range(devices.bit_length() - 1)]
    bits = bits[NEAR:] + bits[:NEAR]
    done = 0
    moved = [shifted(part[0], -1) for part in backs]
    for n in range(1, depth + 1):
        for bit in bits[done : done + TURNS[n - 1]]:
            gains = gains + lax.ppermute(gains, AXES, [(i, i ^ bit) for i in range(devices)])
        done += TURNS[n - 1]
        if n < depth:
            sent = [add(arrived, part[n]) for arrived, part in zip(moved, backs)]
            gains = after(gains, sent[0])
            sent[-1] = after(sent[-1], gains) if RINGS > 1 else sent[-1]
            moved = [shifted(x, -1) for x in sent]
    key_grad, value_grad = finish(
        [(arrived, part[depth]) for arrived, part in zip(moved, backs)], keys, mod_lanes, key_gains
    )
    per_kv = gains.reshape(kv_heads, 8, 2, HD)
    repeat = width // HD // kv_heads
    query_gain = jnp.transpose(per_kv[:, :repeat], (2, 0, 1, 3)).reshape(2, -1)
    key_gain = jnp.transpose(per_kv[:, repeat], (1, 0, 2)).reshape(2, -1)
    return attended, query_grad, key_grad, value_grad, query_gain, key_gain


def solution(mesh):
    rows = P(AXES, None)
    return jax.shard_map(
        on_device,
        mesh=mesh,
        in_specs=(rows, rows, rows, P(AXES), P(), P(), P(), rows),
        out_specs=(rows, rows, rows, rows, P(), P()),
        check_vma=False,
    )
```

```python
import functools
import math

import jax
import jax.numpy as jnp
from jax import lax
from jax.experimental import pallas as pl
from jax.experimental.pallas import tpu as pltpu
from jax.sharding import PartitionSpec as P

HD = 128
MOST = 512
EPS = 1e-06
AXES = ("seq", "head")
CHUNKS = 2
NEAR = 3
TURNS = (2, 2, 2, 2)
RINGS = 2
PRE = False
TIEB = True
EARLY = True
VMEM = 62 * 1024 * 1024
COST = 1
SLAB = 4
FAR = -1e30


def shifted(value, steps):
    count = lax.axis_size(AXES)
    first, last = (max(0, -steps), min(count, count - steps))
    return lax.ppermute(value, AXES, [(source, source + steps) for source in range(first, last)])


def clip_start(clip_lengths, positions):
    order = jnp.arange(clip_lengths.shape[0], dtype=jnp.int32)
    begins = jnp.sum(jnp.where(order[None, :] < order[:, None], clip_lengths[None, :], 0), axis=1)
    chosen = jnp.where(
        begins[None, :] <= positions[:, None], begins[None, :], jnp.zeros((), jnp.int32)
    )
    return jnp.max(chosen, axis=1)


def nn(a, b):
    return lax.dot_general(a, b, (((1,), (0,)), ((), ())), preferred_element_type=jnp.float32)


def nt(a, b):
    return lax.dot_general(a, b, (((1,), (1,)), ((), ())), preferred_element_type=jnp.float32)


def attend_kernel(depth, repeat, skip, *refs):
    blocks = depth + 1
    starts, mod_row, queries, grads, query_gain, key_gain = refs[:6]
    key_refs = refs[6 : 6 + blocks]
    value_refs = refs[6 + blocks : 6 + 2 * blocks]
    mod_refs = refs[6 + 2 * blocks : 6 + 3 * blocks]
    rest = refs[6 + 3 * blocks + skip :]
    attended, query_back = rest[:2]
    back_refs = rest[2 : 2 + blocks]
    sums, bias, kinds = rest[2 + blocks :]
    rows = queries.shape[0]
    span = blocks * rows
    scale = 1.0 / math.sqrt(HD)
    width = SLAB * HD

    @pl.when(pl.program_id(0) == 0)
    def _():
        key_at = lax.broadcasted_iota(jnp.int32, (span, rows), 0)
        query_at = lax.broadcasted_iota(jnp.int32, (span, rows), 1) + depth * rows
        allowed = (key_at >= starts[...]) & (key_at <= query_at)
        bias[...] = jnp.where(allowed, 0.0, FAR)
        for n, ref in enumerate(mod_refs):
            row = ref[...].astype(jnp.float32)[0:1, :]
            kinds[n * rows : (n + 1) * rows, :] = jnp.broadcast_to(row, (HD, rows)).T

    key_raw = jnp.concatenate([r[...] for r in key_refs], 0).astype(jnp.float32)
    key_factor = lax.rsqrt(jnp.mean(key_raw * key_raw, axis=1, keepdims=True) + EPS)
    key_unit = key_raw * key_factor
    key_mod = kinds[...] > 0.5
    own_mod = kinds[depth * rows :, :] > 0.5
    key_norm = (key_unit * jnp.where(key_mod, key_gain[1:2, :], key_gain[0:1, :])).astype(
        jnp.bfloat16
    )
    value = jnp.concatenate([r[...] for r in value_refs], 0)
    key_turned = key_norm.T
    value_turned = value.T
    motion = mod_row[...] == 1

    sums[8:16, :] = jnp.zeros((8, HD), jnp.float32)
    key_acc = None
    value_acc = None
    for slab in range(repeat // SLAB):
        heads = [slab * SLAB + n for n in range(SLAB)]

        def turned(ref):
            return jnp.concatenate(
                [ref[:, h * HD : (h + 1) * HD].astype(jnp.float32).T for h in heads], 1
            )

        raw = turned(queries)
        grad = turned(grads)
        grad_low = grad.astype(jnp.bfloat16)
        factor = lax.rsqrt(jnp.mean(raw * raw, axis=0, keepdims=True) + EPS)
        unit = raw * factor
        gain = jnp.concatenate(
            [
                jnp.where(
                    motion,
                    query_gain[h * HD : (h + 1) * HD, 1:2],
                    query_gain[h * HD : (h + 1) * HD, 0:1],
                )
                for h in heads
            ],
            1,
        )
        query_norm = (unit * gain).astype(jnp.bfloat16)
        shield = jnp.concatenate([bias[...]] * SLAB, 1)
        scores = nn(key_norm, query_norm) * (scale * math.log2(math.e)) + shield
        expo = jnp.exp2(scores - jnp.max(scores, axis=0, keepdims=True))
        probs = expo * (1.0 / jnp.sum(expo, axis=0, keepdims=True))
        probs_low = probs.astype(jnp.bfloat16)
        seen = nn(value_turned, probs_low).astype(jnp.bfloat16)
        seen_wide = seen.astype(jnp.float32)
        delta = jnp.sum(grad * seen_wide, axis=0, keepdims=True)
        prob_grad = nn(value, grad_low)
        score_grad = (probs * (prob_grad - delta) * scale).astype(jnp.bfloat16)
        low = nn(key_turned, score_grad).astype(jnp.bfloat16).astype(jnp.float32)
        along = low * gain
        back = factor * (along - unit * jnp.mean(along * unit, axis=0, keepdims=True))
        term = low * unit
        for n, h in enumerate(heads):
            part = slice(n * HD, (n + 1) * HD)
            cols = slice(h * HD, (h + 1) * HD)
            attended[:, cols] = seen_wide[:, part].T.astype(jnp.bfloat16)
            query_back[:, cols] = back[:, part].T.astype(jnp.bfloat16)
            turn = term[:, part].T
            sums[2 * h : 2 * h + 1, :] = jnp.sum(jnp.where(own_mod, 0.0, turn), axis=0, keepdims=True)
            sums[2 * h + 1 : 2 * h + 2, :] = jnp.sum(jnp.where(own_mod, turn, 0.0), axis=0, keepdims=True)
        key_step = nt(score_grad, query_norm)
        value_step = nt(probs_low, grad_low)
        key_acc = key_step if key_acc is None else key_acc + key_step
        value_acc = value_step if value_acc is None else value_acc + value_step

    for n, ref in enumerate(back_refs):
        part = slice(n * rows, (n + 1) * rows)
        ref[:, :HD] = key_acc[part].astype(ref.dtype)
        ref[:, HD:] = value_acc[part].astype(ref.dtype)
    term = key_acc * key_unit
    of_motion = jnp.sum(jnp.where(key_mod, term, 0.0), axis=0, keepdims=True)
    of_text = jnp.sum(jnp.where(key_mod, 0.0, term), axis=0, keepdims=True)
    sums[2 * repeat : 2 * repeat + 1, :] = of_text
    sums[2 * repeat + 1 : 2 * repeat + 2, :] = of_motion


def attend(first_head, chunk_kv, starts, mod_row, queries, grads, query_gain, key_gain, held, mods, before, wide):
    rows, width = queries.shape
    kv_heads = key_gain.shape[1] // HD
    repeat = width // HD // kv_heads
    blocks = len(held)
    group = repeat * HD

    def at(shape, index):
        return pl.BlockSpec(shape, index)

    whole = lambda g: (0, 0)
    here = lambda g: (0, first_head + g)
    down = lambda g: (first_head + g, 0)
    local = here if wide else lambda g: (0, g)
    mod_at = mods[0].shape[0] // 16 - 1
    in_specs = [
        at((1, rows), whole),
        at((1, rows), whole),
        at((rows, group), here),
        at((rows, group), here),
        at((group, 2), down),
        at((2, HD), here),
    ]
    in_specs += [at((rows, HD), lambda g: (g, 0))] * blocks
    in_specs += [at((rows, HD), lambda g: (chunk_kv + g, 0))] * blocks
    in_specs += [at((16, HD), lambda g: (mod_at, 0))] * blocks
    operands = [starts, mod_row, queries, grads, query_gain, key_gain, *held, *held, *mods]
    aliases = {}
    for n, x in enumerate(before):
        if x is not None:
            aliases[len(operands)] = n
            operands.append(x)
    in_specs += [pl.BlockSpec(memory_space=pl.ANY)] * len(aliases)
    big = jax.ShapeDtypeStruct((rows, width), jnp.bfloat16)
    pair = lambda dtype: jax.ShapeDtypeStruct((rows, (kv_heads if wide else chunk_kv) * 2 * HD), dtype)
    outs = [big, big, pair(jnp.bfloat16)] + [pair(jnp.float32)] * (blocks - 1)
    outs += [jax.ShapeDtypeStruct((kv_heads * 16, HD), jnp.float32)]
    out_specs = [at((rows, group), here)] * 2
    out_specs += [at((rows, 2 * HD), local)] * blocks
    out_specs += [at((16, HD), down)]
    return pl.pallas_call(
        functools.partial(attend_kernel, blocks - 1, repeat, len(aliases)),
        grid=(chunk_kv,),
        in_specs=in_specs,
        out_specs=out_specs,
        out_shape=outs,
        scratch_shapes=[
            pltpu.VMEM((blocks * rows, rows), jnp.float32),
            pltpu.VMEM((blocks * rows, HD), jnp.float32),
        ],
        input_output_aliases=aliases,
        compiler_params=pltpu.CompilerParams(vmem_limit_bytes=VMEM),
        cost_estimate=pl.CostEstimate(
            flops=COST * chunk_kv * repeat * 12 * rows * blocks * rows * HD,
            bytes_accessed=chunk_kv * group * rows * 8 + blocks * rows * chunk_kv * HD * 12,
            transcendentals=chunk_kv * repeat * rows * blocks * rows,
        ),
        name="attend",
    )(*operands)


def finish_kernel(*refs):
    pairs, (keys, mod, key_gain, key_back, value_back) = refs[:-5], refs[-5:]
    motion = mod[...].astype(jnp.float32) > 0.5
    kv_heads = keys.shape[1] // HD
    kv = kv_heads // (len(pairs) // 2)
    for g in range(kv_heads):
        arrived, own = pairs[2 * (g // kv) : 2 * (g // kv) + 2]
        cols = slice(g * HD, (g + 1) * HD)
        at = 2 * (g % kv) * HD
        both = arrived[:, at : at + 2 * HD].astype(jnp.float32) + own[:, at : at + 2 * HD]
        low = both[:, :HD].astype(jnp.bfloat16).astype(jnp.float32)
        raw = keys[:, cols].astype(jnp.float32)
        factor = lax.rsqrt(jnp.mean(raw * raw, axis=1, keepdims=True) + EPS)
        unit = raw * factor
        along = low * jnp.where(motion, key_gain[1:2, cols], key_gain[0:1, cols])
        back = factor * (along - unit * jnp.mean(along * unit, axis=1, keepdims=True))
        key_back[:, cols] = back.astype(jnp.bfloat16)
        value_back[:, cols] = both[:, HD:].astype(jnp.bfloat16)


def finish(pairs, keys, mod_lanes, key_gain):
    low = jax.ShapeDtypeStruct(keys.shape, jnp.bfloat16)
    full = lambda x: pl.BlockSpec(x.shape, lambda g: (0, 0))
    operands = [x for pair in pairs for x in pair] + [keys, mod_lanes, key_gain]
    return pl.pallas_call(
        finish_kernel,
        grid=(1,),
        in_specs=[full(x) for x in operands],
        out_specs=[full(keys)] * 2,
        out_shape=[low, low],
        compiler_params=pltpu.CompilerParams(vmem_limit_bytes=VMEM),
        name="finish",
    )(*operands)


def after(value, *others):
    return lax.optimization_barrier((value, *others))[0]


def on_device(queries, keys, values, modality, clip_lengths, query_gains, key_gains, out_grad):
    count, width = queries.shape
    devices = lax.axis_size(AXES)
    kv_heads = keys.shape[1] // HD
    kv = kv_heads // CHUNKS
    depth = (MOST + count - 1) // count
    first = lax.axis_index(AXES) * count
    mod_lanes = jnp.broadcast_to(modality.astype(jnp.bfloat16)[:, None], (count, HD))
    mod_rows = jnp.broadcast_to(modality.astype(jnp.bfloat16)[None, :], (16, count))

    def payload(chunk):
        heads = range(chunk * kv, (chunk + 1) * kv)
        blocks = [x[:, h * HD : (h + 1) * HD] for x in (keys, values) for h in heads]
        return jnp.concatenate(blocks + ([mod_rows] if chunk == 0 else []), 0)

    starts = clip_start(clip_lengths, first + jnp.arange(count, dtype=jnp.int32))
    starts = (starts - first + depth * count)[None, :]
    gain_columns = query_gains.T
    ahead = [payload(0)]
    behind = [payload(1)]
    for n in range(depth):
        ahead.append(shifted(after(ahead[-1], gain_columns, starts) if EARLY and n == 2 else ahead[-1], 1))
        behind.append(shifted(behind[-1], 1))
    mods = ahead[::-1]

    mod_row = modality[None, :]

    def add(arrived, part):
        return (arrived.astype(jnp.float32) + part).astype(jnp.bfloat16)

    outs = [None] * (depth + 4)
    backs = []
    for chunk, held in enumerate((ahead, behind)):
        if RINGS > 1:
            outs = [*outs[:2], *[None] * (depth + 1), outs[-1]]
        outs = attend(
            chunk * kv,
            kv,
            starts,
            mod_row,
            queries,
            out_grad,
            gain_columns,
            key_gains,
            held[::-1],
            mods,
            outs,
            RINGS == 1,
        )
        backs.append(outs[2:-1])
    backs = backs[-RINGS:]
    attended, query_grad = outs[:2]
    gains = outs[-1]
    bits = [1 << n for n in range(devices.bit_length() - 1)]
    bits = bits[NEAR:] + bits[:NEAR]
    moved = [shifted(part[0], -1) for part in backs]
    if PRE:
        gains = after(gains, moved[0])
    for n in range(1, depth + 1):
        if n < depth:
            sent = [add(arrived, part[n]) for arrived, part in zip(moved, backs)]
            if PRE:
                gains = after(gains, sent[0])
        for _ in range(TURNS[n - 1]):
            bit = bits.pop(0)
            gains = gains + lax.ppermute(gains, AXES, [(i, i ^ bit) for i in range(devices)])
        if n < depth:
            if not PRE:
                gains = after(gains, sent[0])
            if TIEB:
                sent[-1] = after(sent[-1], gains)
            moved = [shifted(x, -1) for x in sent]
    key_grad, value_grad = finish(
        [(arrived, part[depth]) for arrived, part in zip(moved, backs)], keys, mod_lanes, key_gains
    )
    per_kv = gains.reshape(kv_heads, 8, 2, HD)
    repeat = width // HD // kv_heads
    query_gain = jnp.transpose(per_kv[:, :repeat], (2, 0, 1, 3)).reshape(2, -1)
    key_gain = jnp.transpose(per_kv[:, repeat], (1, 0, 2)).reshape(2, -1)
    return attended, query_grad, key_grad, value_grad, query_gain, key_gain


def solution(mesh):
    rows = P(AXES, None)
    return jax.shard_map(
        on_device,
        mesh=mesh,
        in_specs=(rows, rows, rows, P(AXES), P(), P(), P(), rows),
        out_specs=(rows, rows, rows, rows, P(), P()),
        check_vma=False,
    )
```

```python
import functools
import math

import jax
import jax.numpy as jnp
from jax import lax
from jax.experimental import pallas as pl
from jax.experimental.pallas import tpu as pltpu
from jax.sharding import PartitionSpec as P

HD = 128
MOST = 512
EPS = 1e-06
AXES = ("seq", "head")
CHUNKS = 2
NEAR = 3
TURNS = (2, 2, 2, 2)
RINGS = 2
PRE = False
TIEB = True
EARLY = True
VMEM = 62 * 1024 * 1024
COST = 1
SLAB = 4
FAR = -1e30


def shifted(value, steps):
    count = lax.axis_size(AXES)
    first, last = (max(0, -steps), min(count, count - steps))
    return lax.ppermute(value, AXES, [(source, source + steps) for source in range(first, last)])


def clip_start(clip_lengths, positions):
    order = jnp.arange(clip_lengths.shape[0], dtype=jnp.int32)
    begins = jnp.sum(jnp.where(order[None, :] < order[:, None], clip_lengths[None, :], 0), axis=1)
    chosen = jnp.where(
        begins[None, :] <= positions[:, None], begins[None, :], jnp.zeros((), jnp.int32)
    )
    return jnp.max(chosen, axis=1)


def nn(a, b):
    return lax.dot_general(a, b, (((1,), (0,)), ((), ())), preferred_element_type=jnp.float32)


def nt(a, b):
    return lax.dot_general(a, b, (((1,), (1,)), ((), ())), preferred_element_type=jnp.float32)


def attend_kernel(depth, repeat, skip, *refs):
    blocks = depth + 1
    starts, mod_row, queries, grads, query_gain, key_gain = refs[:6]
    key_refs = refs[6 : 6 + blocks]
    value_refs = refs[6 + blocks : 6 + 2 * blocks]
    mod_refs = refs[6 + 2 * blocks : 6 + 3 * blocks]
    rest = refs[6 + 3 * blocks + skip :]
    attended, query_back = rest[:2]
    back_refs = rest[2 : 2 + blocks]
    sums, bias, kinds = rest[2 + blocks :]
    rows = queries.shape[0]
    span = blocks * rows
    scale = 1.0 / math.sqrt(HD)
    width = SLAB * HD

    @pl.when(pl.program_id(0) == 0)
    def _():
        key_at = lax.broadcasted_iota(jnp.int32, (span, rows), 0)
        query_at = lax.broadcasted_iota(jnp.int32, (span, rows), 1) + depth * rows
        allowed = (key_at >= starts[...]) & (key_at <= query_at)
        bias[...] = jnp.where(allowed, 0.0, FAR)
        for n, ref in enumerate(mod_refs):
            row = ref[...].astype(jnp.float32)[0:1, :]
            kinds[n * rows : (n + 1) * rows, :] = jnp.broadcast_to(row, (HD, rows)).T

    key_raw = jnp.concatenate([r[...] for r in key_refs], 0).astype(jnp.float32)
    key_factor = lax.rsqrt(jnp.mean(key_raw * key_raw, axis=1, keepdims=True) + EPS)
    key_unit = key_raw * key_factor
    key_mod = kinds[...] > 0.5
    own_mod = kinds[depth * rows :, :] > 0.5
    key_norm = (key_unit * jnp.where(key_mod, key_gain[1:2, :], key_gain[0:1, :])).astype(
        jnp.bfloat16
    )
    value = jnp.concatenate([r[...] for r in value_refs], 0)
    key_turned = key_norm.T
    value_turned = value.T
    motion = mod_row[...] == 1

    sums[8:16, :] = jnp.zeros((8, HD), jnp.float32)
    key_acc = None
    value_acc = None
    for slab in range(repeat // SLAB):
        heads = [slab * SLAB + n for n in range(SLAB)]

        def turned(ref):
            return jnp.concatenate(
                [ref[:, h * HD : (h + 1) * HD].astype(jnp.float32).T for h in heads], 1
            )

        raw = turned(queries)
        grad = turned(grads)
        grad_low = grad.astype(jnp.bfloat16)
        factor = lax.rsqrt(jnp.mean(raw * raw, axis=0, keepdims=True) + EPS)
        unit = raw * factor
        gain = jnp.concatenate(
            [
                jnp.where(
                    motion,
                    query_gain[h * HD : (h + 1) * HD, 1:2],
                    query_gain[h * HD : (h + 1) * HD, 0:1],
                )
                for h in heads
            ],
            1,
        )
        query_norm = (unit * gain).astype(jnp.bfloat16)
        shield = jnp.concatenate([bias[...]] * SLAB, 1)
        scores = nn(key_norm, query_norm) * (scale * math.log2(math.e)) + shield
        expo = jnp.exp2(scores - jnp.max(scores, axis=0, keepdims=True))
        probs = expo * (1.0 / jnp.sum(expo, axis=0, keepdims=True))
        probs_low = probs.astype(jnp.bfloat16)
        seen = nn(value_turned, probs_low).astype(jnp.bfloat16)
        seen_wide = seen.astype(jnp.float32)
        delta = jnp.sum(grad * seen_wide, axis=0, keepdims=True)
        prob_grad = nn(value, grad_low)
        score_grad = (probs * (prob_grad - delta) * scale).astype(jnp.bfloat16)
        low = nn(key_turned, score_grad).astype(jnp.bfloat16).astype(jnp.float32)
        along = low * gain
        back = factor * (along - unit * jnp.mean(along * unit, axis=0, keepdims=True))
        term = low * unit
        for n, h in enumerate(heads):
            part = slice(n * HD, (n + 1) * HD)
            cols = slice(h * HD, (h + 1) * HD)
            attended[:, cols] = seen_wide[:, part].T.astype(jnp.bfloat16)
            query_back[:, cols] = back[:, part].T.astype(jnp.bfloat16)
            turn = term[:, part].T
            sums[2 * h : 2 * h + 1, :] = jnp.sum(jnp.where(own_mod, 0.0, turn), axis=0, keepdims=True)
            sums[2 * h + 1 : 2 * h + 2, :] = jnp.sum(jnp.where(own_mod, turn, 0.0), axis=0, keepdims=True)
        key_step = nt(score_grad, query_norm)
        value_step = nt(probs_low, grad_low)
        key_acc = key_step if key_acc is None else key_acc + key_step
        value_acc = value_step if value_acc is None else value_acc + value_step

    for n, ref in enumerate(back_refs):
        part = slice(n * rows, (n + 1) * rows)
        ref[:, :HD] = key_acc[part].astype(ref.dtype)
        ref[:, HD:] = value_acc[part].astype(ref.dtype)
    term = key_acc * key_unit
    of_motion = jnp.sum(jnp.where(key_mod, term, 0.0), axis=0, keepdims=True)
    of_text = jnp.sum(jnp.where(key_mod, 0.0, term), axis=0, keepdims=True)
    sums[2 * repeat : 2 * repeat + 1, :] = of_text
    sums[2 * repeat + 1 : 2 * repeat + 2, :] = of_motion


def attend(first_head, chunk_kv, starts, mod_row, queries, grads, query_gain, key_gain, held, mods, before, wide):
    rows, width = queries.shape
    kv_heads = key_gain.shape[1] // HD
    repeat = width // HD // kv_heads
    blocks = len(held)
    group = repeat * HD

    def at(shape, index):
        return pl.BlockSpec(shape, index)

    whole = lambda g: (0, 0)
    here = lambda g: (0, first_head + g)
    down = lambda g: (first_head + g, 0)
    local = here if wide else lambda g: (0, g)
    mod_at = mods[0].shape[0] // 16 - 1
    in_specs = [
        at((1, rows), whole),
        at((1, rows), whole),
        at((rows, group), here),
        at((rows, group), here),
        at((group, 2), down),
        at((2, HD), here),
    ]
    in_specs += [at((rows, HD), lambda g: (g, 0))] * blocks
    in_specs += [at((rows, HD), lambda g: (chunk_kv + g, 0))] * blocks
    in_specs += [at((16, HD), lambda g: (mod_at, 0))] * blocks
    operands = [starts, mod_row, queries, grads, query_gain, key_gain, *held, *held, *mods]
    aliases = {}
    for n, x in enumerate(before):
        if x is not None:
            aliases[len(operands)] = n
            operands.append(x)
    in_specs += [pl.BlockSpec(memory_space=pl.ANY)] * len(aliases)
    big = jax.ShapeDtypeStruct((rows, width), jnp.bfloat16)
    pair = lambda dtype: jax.ShapeDtypeStruct((rows, (kv_heads if wide else chunk_kv) * 2 * HD), dtype)
    outs = [big, big, pair(jnp.bfloat16)] + [pair(jnp.float32)] * (blocks - 1)
    outs += [jax.ShapeDtypeStruct((kv_heads * 16, HD), jnp.float32)]
    out_specs = [at((rows, group), here)] * 2
    out_specs += [at((rows, 2 * HD), local)] * blocks
    out_specs += [at((16, HD), down)]
    return pl.pallas_call(
        functools.partial(attend_kernel, blocks - 1, repeat, len(aliases)),
        grid=(chunk_kv,),
        in_specs=in_specs,
        out_specs=out_specs,
        out_shape=outs,
        scratch_shapes=[
            pltpu.VMEM((blocks * rows, rows), jnp.float32),
            pltpu.VMEM((blocks * rows, HD), jnp.float32),
        ],
        input_output_aliases=aliases,
        compiler_params=pltpu.CompilerParams(vmem_limit_bytes=VMEM),
        cost_estimate=pl.CostEstimate(
            flops=COST * chunk_kv * repeat * 12 * rows * blocks * rows * HD,
            bytes_accessed=chunk_kv * group * rows * 8 + blocks * rows * chunk_kv * HD * 12,
            transcendentals=chunk_kv * repeat * rows * blocks * rows,
        ),
        name="attend",
    )(*operands)


def finish_kernel(*refs):
    pairs, (keys, mod, key_gain, key_back, value_back) = refs[:-5], refs[-5:]
    motion = mod[...].astype(jnp.float32) > 0.5
    kv_heads = keys.shape[1] // HD
    kv = kv_heads // (len(pairs) // 2)
    for g in range(kv_heads):
        arrived, own = pairs[2 * (g // kv) : 2 * (g // kv) + 2]
        cols = slice(g * HD, (g + 1) * HD)
        at = 2 * (g % kv) * HD
        both = arrived[:, at : at + 2 * HD].astype(jnp.float32) + own[:, at : at + 2 * HD]
        low = both[:, :HD].astype(jnp.bfloat16).astype(jnp.float32)
        raw = keys[:, cols].astype(jnp.float32)
        factor = lax.rsqrt(jnp.mean(raw * raw, axis=1, keepdims=True) + EPS)
        unit = raw * factor
        along = low * jnp.where(motion, key_gain[1:2, cols], key_gain[0:1, cols])
        back = factor * (along - unit * jnp.mean(along * unit, axis=1, keepdims=True))
        key_back[:, cols] = back.astype(jnp.bfloat16)
        value_back[:, cols] = both[:, HD:].astype(jnp.bfloat16)


def finish(pairs, keys, mod_lanes, key_gain):
    low = jax.ShapeDtypeStruct(keys.shape, jnp.bfloat16)
    full = lambda x: pl.BlockSpec(x.shape, lambda g: (0, 0))
    operands = [x for pair in pairs for x in pair] + [keys, mod_lanes, key_gain]
    return pl.pallas_call(
        finish_kernel,
        grid=(1,),
        in_specs=[full(x) for x in operands],
        out_specs=[full(keys)] * 2,
        out_shape=[low, low],
        compiler_params=pltpu.CompilerParams(vmem_limit_bytes=VMEM),
        name="finish",
    )(*operands)


def after(value, *others):
    return lax.optimization_barrier((value, *others))[0]


def on_device(queries, keys, values, modality, clip_lengths, query_gains, key_gains, out_grad):
    count, width = queries.shape
    devices = lax.axis_size(AXES)
    kv_heads = keys.shape[1] // HD
    kv = kv_heads // CHUNKS
    depth = (MOST + count - 1) // count
    first = lax.axis_index(AXES) * count
    mod_lanes = jnp.broadcast_to(modality.astype(jnp.bfloat16)[:, None], (count, HD))
    mod_rows = jnp.broadcast_to(modality.astype(jnp.bfloat16)[None, :], (16, count))

    def payload(chunk):
        heads = range(chunk * kv, (chunk + 1) * kv)
        blocks = [x[:, h * HD : (h + 1) * HD] for x in (keys, values) for h in heads]
        return jnp.concatenate(blocks + ([mod_rows] if chunk == 0 else []), 0)

    starts = clip_start(clip_lengths, first + jnp.arange(count, dtype=jnp.int32))
    starts = (starts - first + depth * count)[None, :]
    gain_columns = query_gains.T
    ahead = [payload(0)]
    behind = [payload(1)]
    for n in range(depth):
        ahead.append(shifted(after(ahead[-1], gain_columns, starts) if EARLY and n == 2 else ahead[-1], 1))
        behind.append(shifted(behind[-1], 1))
    mods = ahead[::-1]

    mod_row = modality[None, :]

    def add(arrived, part):
        return (arrived.astype(jnp.float32) + part).astype(jnp.bfloat16)

    outs = [None] * (depth + 4)
    backs = []
    for chunk, held in enumerate((ahead, behind)):
        if RINGS > 1:
            outs = [*outs[:2], *[None] * (depth + 1), outs[-1]]
        outs = attend(
            chunk * kv,
            kv,
            starts,
            mod_row,
            queries,
            out_grad,
            gain_columns,
            key_gains,
            held[::-1],
            mods,
            outs,
            RINGS == 1,
        )
        backs.append(outs[2:-1])
    backs = backs[-RINGS:]
    attended, query_grad = outs[:2]
    gains = outs[-1]
    bits = [1 << n for n in range(devices.bit_length() - 1)]
    bits = bits[NEAR:] + bits[:NEAR][::-1]
    moved = [shifted(part[0], -1) for part in backs]
    if PRE:
        gains = after(gains, moved[0])
    for n in range(1, depth + 1):
        if n < depth:
            sent = [add(arrived, part[n]) for arrived, part in zip(moved, backs)]
            if PRE:
                gains = after(gains, sent[0])
        for _ in range(TURNS[n - 1]):
            bit = bits.pop(0)
            gains = gains + lax.ppermute(gains, AXES, [(i, i ^ bit) for i in range(devices)])
        if n < depth:
            if not PRE:
                gains = after(gains, sent[0])
            if TIEB:
                sent[-1] = after(sent[-1], gains)
            moved = [shifted(x, -1) for x in sent]
    key_grad, value_grad = finish(
        [(arrived, part[depth]) for arrived, part in zip(moved, backs)], keys, mod_lanes, key_gains
    )
    per_kv = gains.reshape(kv_heads, 8, 2, HD)
    repeat = width // HD // kv_heads
    query_gain = jnp.transpose(per_kv[:, :repeat], (2, 0, 1, 3)).reshape(2, -1)
    key_gain = jnp.transpose(per_kv[:, repeat], (1, 0, 2)).reshape(2, -1)
    return attended, query_grad, key_grad, value_grad, query_gain, key_gain


def solution(mesh):
    rows = P(AXES, None)
    return jax.shard_map(
        on_device,
        mesh=mesh,
        in_specs=(rows, rows, rows, P(AXES), P(), P(), P(), rows),
        out_specs=(rows, rows, rows, rows, P(), P()),
        check_vma=False,
    )
```
